32 devices in a mesh: adv: 16 (over z, y, core), imp: 2 (over x).
Axes of the slice: x: 2, y: 2, z: 4, core: 2. Of those that a mesh axis runs over, the one named last changes fastest.
Arguments:
- values: bfloat16 [4096, 16384], P('adv', 'imp'), may hold values from 0 to 4
- limits: float32 [4096], P('adv'), may hold values from 0.05 to 3
- start_pace: float32 [4096], P('adv'), may hold values from 0.3 to 1
- reserve: float32 [16384], P('imp'), may hold values from 0.2 to 1.2
Outputs:
- pace: float32 [4096], P('adv')
- prices: float32 [16384], P('imp')
The draws below stay inside these ranges and needn't reach their ends.
All inputs are finite; a program needn't handle non-finite values.
Results may differ from the reference program's by a relative error of at most 0.0003.
Values sent between devices are 32-bit elements; how exact they have to be, the bound alone decides.
A program may use at most 64 MiB of HBM per device.

```python
import math
import jax
import jax.numpy as jnp
from jax import lax

M = 16384
ROUNDS = 2
A = 4096


def draw_values(key, part):
    first = jax.random.fold_in(jax.random.fold_in(key, 7), 0)
    column = 1.0 + 2.0 * jnp.arange(M, dtype=jnp.float32) / M
    base = jnp.exp(jax.random.uniform(first, (A, M), jnp.float32, -3.0, 0.0)) * column[None, :]
    return base.astype(jnp.bfloat16)


def level_of(key, dims, cuts, least, largest):
    loudness = 1.0
    for axis_at, blocks in cuts:
        draws = jax.random.uniform(jax.random.fold_in(jax.random.fold_in(key, 6), axis_at), (blocks,), jnp.float32, least / len(cuts), largest / len(cuts))
        loudness = loudness * jnp.repeat(jnp.exp(draws), dims[axis_at] // blocks).reshape((-1,) + (1,) * (len(dims) - 1 - axis_at))
    return loudness


def setup_inputs(seed: int = 0) -> dict:
    key_list = jax.random.split(jax.random.key(seed), 5)
    values = draw_values(jax.random.fold_in(key_list[4], 71), 0)
    limits = jnp.clip(jnp.exp(math.log(3.0) - 4.0943445 * jax.random.uniform(key_list[1], (A,), jnp.float32) ** level_of(key_list[1], (A,), ((0, 16),), -0.2, 0.2)), 0.05, 3.0)
    start_pace = jnp.clip(jnp.exp(math.log(1.0) - 1.2039728 * jax.random.uniform(key_list[2], (A,), jnp.float32) ** level_of(key_list[2], (A,), ((0, 16),), -0.2, 0.2)), 0.3, 1.0)
    reserve = jnp.clip(0.2 + 1 * jax.random.uniform(key_list[3], (M,), jnp.float32) ** level_of(key_list[3], (M,), ((0, 2),), -0.2, 0.2), 0.2, 1.2)
    return dict(values=values, limits=limits, start_pace=start_pace, reserve=reserve)


EPS = 0.015

def one_round(values, pace, limits, reserve):
    width = min(512, M)
    starts = (jnp.arange(M // width) * width).astype(jnp.int32)

    def block(spend, start):
        cols = lax.dynamic_slice_in_dim(values, start, width, 1).astype(jnp.float32)
        rlog = lax.dynamic_slice_in_dim(reserve, start, width, 0) / EPS
        bid = pace[:, None] * cols
        score = bid / EPS
        top = jnp.maximum(lax.optimization_barrier(jnp.max(score, axis=0)), rlog)
        total = lax.optimization_barrier(jnp.sum(jnp.exp(score - top[None, :]), axis=0)) + jnp.exp(rlog - top)
        lse = top + jnp.log(total)
        share = jnp.exp(score - lse[None, :])
        return (spend + lax.optimization_barrier(jnp.sum(share * bid, axis=1)), EPS * lse)
    spend, prices = lax.scan(block, jnp.zeros((values.shape[0],), jnp.float32), starts)
    new_pace = jnp.minimum(1.0, pace * jnp.sqrt(limits / spend))
    return (new_pace, prices.reshape(M))

def reference(values, limits, start_pace, reserve):
    pace = start_pace
    prices = jnp.zeros((M,), jnp.float32)
    for step in range(ROUNDS):
        pace, prices = one_round(values, pace, limits, reserve)
    return (pace, prices)
```

```python
import functools
import math

import jax
import jax.numpy as jnp
from jax import lax
from jax.experimental import pallas as pl
from jax.experimental.pallas import tpu as pltpu
from jax.sharding import PartitionSpec as P

ROUNDS = 2
EPS = 0.015
LANES = 128
LOG2E = math.log2(math.e)
LN2 = math.log(2.0)
SCALE = LOG2E / EPS


def kernel(
    n, m, owners,
    values, limits, start, reserve,
    pace_out, price_out,
    held, weighted, column, column16, pace_row, tops, sums, mine, parts, lses, spends,
    load_sem, send_part, recv_part, send_lse, recv_lse, send_spend, recv_spend,
):
    adv, imp = lax.axis_index("adv"), lax.axis_index("imp")
    stride = n // owners
    base = adv // stride
    segs, rows, width = held.shape
    wide = width // LANES
    halves = rows // LANES

    def load(k):
        return pltpu.make_async_copy(
            values.at[:, pl.ds(pl.multiple_of(k * width, width), width)], held.at[k], load_sem.at[k]
        )

    def part_copy(step, k, source, target):
        return pltpu.make_async_remote_copy(
            src_ref=mine.at[step, k], dst_ref=parts.at[step, source],
            send_sem=send_part.at[step, k], recv_sem=recv_part.at[step, source],
            device_id=(target, imp), device_id_type=pl.DeviceIdType.MESH,
        )

    def lse_copy(step, k, target):
        return pltpu.make_async_remote_copy(
            src_ref=lses.at[step, k], dst_ref=lses.at[step, k],
            send_sem=send_lse.at[step, target], recv_sem=recv_lse.at[step, k],
            device_id=(target, imp), device_id_type=pl.DeviceIdType.MESH,
        )

    def spend_copy(step, source, target):
        return pltpu.make_async_remote_copy(
            src_ref=spends.at[step, source], dst_ref=spends.at[step, source],
            send_sem=send_spend.at[step, target], recv_sem=recv_spend.at[step, source],
            device_id=(adv, target), device_id_type=pl.DeviceIdType.MESH,
        )

    @pl.loop(0, owners)
    def _(t):
        load(lax.rem(base + 1 + t, owners)).start()

    barrier = pltpu.get_barrier_semaphore()

    @pl.loop(1, n)
    def _(t):
        pl.semaphore_signal(
            barrier, inc=1, device_id=(lax.rem(adv + t, n), imp), device_id_type=pl.DeviceIdType.MESH
        )

    @pl.loop(1, m)
    def _(t):
        pl.semaphore_signal(
            barrier, inc=1, device_id=(adv, lax.rem(imp + t, m)), device_id_type=pl.DeviceIdType.MESH
        )

    def set_column():
        for h in range(halves):
            spread = jnp.broadcast_to(pace_row[h : h + 1, :], (LANES, LANES)).T * SCALE
            column[h * LANES : (h + 1) * LANES, :] = spread
            column16[h * LANES : (h + 1) * LANES, :] = spread.astype(jnp.bfloat16)

    pace_row[...] = start[...]
    set_column()
    pl.semaphore_wait(barrier, n - 1 + m - 1)

    for step in range(ROUNDS):

        @pl.loop(0, owners)
        def _(t):
            k = lax.rem(base + 1 + t, owners)
            if step == 0:
                load(k).wait()
            for r in range(wide):
                lanes = slice(r * LANES, (r + 1) * LANES)
                value = held[k, :, lanes]
                rough = (value * column16[...]).reshape(rows // 16, 16, LANES)
                top = jnp.max(jnp.max(rough, axis=0).astype(jnp.float32), axis=0, keepdims=True)
                value = value.astype(jnp.float32)
                scaled = jnp.exp2(value * column[...] - top)
                tops[k, r : r + 1, :] = top
                sums[r : r + 1, :] = jnp.sum(scaled, axis=0, keepdims=True)
                weighted[k, :, lanes] = scaled * value
            local = tops[k] + jnp.log(sums[...]) * LOG2E
            owner = k * stride

            @pl.when(owner != adv)
            def _():
                mine[step, k] = local
                part_copy(step, k, adv, owner).start()

            @pl.when(owner == adv)
            def _():
                parts[step, adv] = local

        def own():
            @pl.loop(1, n)
            def _(t):
                part_copy(step, base, lax.rem(adv + n - t, n), adv).wait_recv()

            every = parts[step]
            floor = reserve[base] * SCALE
            upper = jnp.maximum(jnp.max(every, axis=0), floor)
            whole = jnp.sum(jnp.exp2(every - upper[None]), axis=0) + jnp.exp2(floor - upper)
            lses[step, base] = upper + jnp.log(whole) * LOG2E

            @pl.loop(1, n)
            def _(t):
                lse_copy(step, base, lax.rem(adv + t, n)).start()

        if stride == 1:
            own()
        else:
            pl.when(base * stride == adv)(own)

        def gather(t, total):
            k = lax.rem(base + owners - t, owners)

            @pl.when(k * stride != adv)
            def _():
                lse_copy(step, k, adv).wait_recv()

            share = jnp.exp2(tops[k] - lses[step, k])
            for r in range(wide):
                total = total + weighted[k, :, r * LANES : (r + 1) * LANES] * share[r : r + 1, :]
            return total

        total = lax.fori_loop(0, owners, gather, jnp.zeros((rows, LANES), jnp.float32))
        for h in range(halves):
            spends[step, imp, h : h + 1, :] = jnp.sum(
                total[h * LANES : (h + 1) * LANES, :].T, axis=0, keepdims=True
            )

        @pl.loop(1, m)
        def _(t):
            spend_copy(step, imp, lax.rem(imp + t, m)).start()

        if step == ROUNDS - 1:
            price_out[...] = lses[step] * (EPS * LN2)

        @pl.loop(1, m)
        def _(t):
            spend_copy(step, lax.rem(imp + t, m), imp).wait_recv()

        spend = pace_row[...] * jnp.sum(spends[step], axis=0)
        pace_row[...] = jnp.minimum(1.0, pace_row[...] * jnp.sqrt(limits[...] / spend))
        if step < ROUNDS - 1:
            set_column()
    pace_out[...] = pace_row[...]

    for step in range(ROUNDS):

        @pl.loop(0, owners)
        def _(k):
            @pl.when(k * stride != adv)
            def _():
                part_copy(step, k, adv, k * stride).wait_send()

        def sent():
            @pl.loop(1, n)
            def _(t):
                lse_copy(step, base, lax.rem(adv + t, n)).wait_send()

        if stride == 1:
            sent()
        else:
            pl.when(base * stride == adv)(sent)

        @pl.loop(1, m)
        def _(t):
            spend_copy(step, imp, lax.rem(imp + t, m)).wait_send()


def on_device(n, m, values, limits, start_pace, reserve):
    rows, columns = values.shape
    tiles = columns // LANES
    owners = math.gcd(n, tiles)
    wide = tiles // owners
    halves = rows // LANES
    vmem = pl.BlockSpec(memory_space=pltpu.VMEM)
    f32 = jnp.float32
    pace, prices = pl.pallas_call(
        functools.partial(kernel, n, m, owners),
        out_shape=(
            jax.ShapeDtypeStruct((halves, LANES), f32),
            jax.ShapeDtypeStruct((owners, wide, LANES), f32),
        ),
        in_specs=[pl.BlockSpec(memory_space=pl.ANY), vmem, vmem, vmem],
        out_specs=(vmem, vmem),
        scratch_shapes=[
            pltpu.VMEM((owners, rows, wide * LANES), jnp.bfloat16),
            pltpu.VMEM((owners, rows, wide * LANES), f32),
            pltpu.VMEM((rows, LANES), f32),
            pltpu.VMEM((rows, LANES), jnp.bfloat16),
            pltpu.VMEM((halves, LANES), f32),
            pltpu.VMEM((owners, wide, LANES), f32),
            pltpu.VMEM((wide, LANES), f32),
            pltpu.VMEM((ROUNDS, owners, wide, LANES), f32),
            pltpu.VMEM((ROUNDS, n, wide, LANES), f32),
            pltpu.VMEM((ROUNDS, owners, wide, LANES), f32),
            pltpu.VMEM((ROUNDS, m, halves, LANES), f32),
            pltpu.SemaphoreType.DMA((owners,)),
            pltpu.SemaphoreType.DMA((ROUNDS, owners)),
            pltpu.SemaphoreType.DMA((ROUNDS, n)),
            pltpu.SemaphoreType.DMA((ROUNDS, n)),
            pltpu.SemaphoreType.DMA((ROUNDS, owners)),
            pltpu.SemaphoreType.DMA((ROUNDS, m)),
            pltpu.SemaphoreType.DMA((ROUNDS, m)),
        ],
        compiler_params=pltpu.CompilerParams(
            collective_id=0, has_side_effects=True, vmem_limit_bytes=62 * 2**20
        ),
        name="pacing",
    )(
        values,
        limits.reshape(halves, LANES),
        start_pace.reshape(halves, LANES),
        reserve.reshape(owners, wide, LANES),
    )
    return pace.reshape(rows), prices.reshape(columns)


def solution(mesh):
    placed = (P("adv", "imp"), P("adv"), P("adv"), P("imp"))
    body = functools.partial(on_device, mesh.shape["adv"], mesh.shape["imp"])
    return jax.shard_map(
        body, mesh=mesh, in_specs=placed, out_specs=(P("adv"), P("imp")), check_vma=False
    )
```

```python
import functools
import math

import jax
import jax.numpy as jnp
from jax import lax
from jax.experimental import pallas as pl
from jax.experimental.pallas import tpu as pltpu
from jax.sharding import PartitionSpec as P

ROUNDS = 2
EPS = 0.015
LANES = 128
BATCH = 4
LOG2E = math.log2(math.e)
LN2 = math.log(2.0)
SCALE = LOG2E / EPS


def kernel(
    n, m, owners,
    values, limits, start, reserve,
    pace_out, price_out,
    held, weighted, column, column16, pace_row, tops, shares, mine, parts, lses, spends,
    load_sem, send_part, recv_part, send_lse, recv_lse, send_spend, recv_spend,
):
    adv, imp = lax.axis_index("adv"), lax.axis_index("imp")
    stride = n // owners
    base = adv // stride
    segs, rows, width = held.shape
    wide = width // LANES
    halves = rows // LANES

    def load(k):
        return pltpu.make_async_copy(
            values.at[:, pl.ds(pl.multiple_of(k * width, width), width)], held.at[k], load_sem.at[k]
        )

    def part_copy(step, k, source, target):
        return pltpu.make_async_remote_copy(
            src_ref=mine.at[step, k], dst_ref=parts.at[step, source],
            send_sem=send_part.at[step], recv_sem=recv_part.at[step],
            device_id=(target, imp), device_id_type=pl.DeviceIdType.MESH,
        )

    def lse_copy(step, k, target):
        return pltpu.make_async_remote_copy(
            src_ref=lses.at[step, k], dst_ref=lses.at[step, k],
            send_sem=send_lse.at[step], recv_sem=recv_lse.at[step],
            device_id=(target, imp), device_id_type=pl.DeviceIdType.MESH,
        )

    def spend_copy(step, source, target):
        return pltpu.make_async_remote_copy(
            src_ref=spends.at[step, source], dst_ref=spends.at[step, source],
            send_sem=send_spend.at[step, target], recv_sem=recv_spend.at[step, source],
            device_id=(adv, target), device_id_type=pl.DeviceIdType.MESH,
        )

    is_owner = base * stride == adv
    batch = math.gcd(owners, BATCH)

    def drain(ref, sem, most):
        def wait(count):
            blocks = ref.at[pl.ds(0, count)]
            pltpu.make_async_copy(blocks, blocks, sem).wait()

        if stride == 1:
            wait(most - 1)
        else:
            pl.when(is_owner)(lambda: wait(most - 1))
            pl.when(jnp.logical_not(is_owner))(lambda: wait(most))

    def if_owner(run):
        if stride == 1:
            run()
        else:
            pl.when(is_owner)(run)

    barrier = pltpu.get_barrier_semaphore()

    @pl.loop(1, n, unroll=True)
    def _(t):
        pl.semaphore_signal(
            barrier, inc=1, device_id=(lax.rem(adv + t, n), imp), device_id_type=pl.DeviceIdType.MESH
        )

    @pl.loop(1, m, unroll=True)
    def _(t):
        pl.semaphore_signal(
            barrier, inc=1, device_id=(adv, lax.rem(imp + t, m)), device_id_type=pl.DeviceIdType.MESH
        )

    @pl.loop(0, owners)
    def _(t):
        load(lax.rem(base + 1 + t, owners)).start()

    def set_column():
        for h in range(halves):
            spread = jnp.broadcast_to(pace_row[h : h + 1, :], (LANES, LANES)).T * SCALE
            column[h * LANES : (h + 1) * LANES, :] = spread
            column16[h * LANES : (h + 1) * LANES, :] = spread.astype(jnp.bfloat16)

    pace_row[...] = start[...]
    set_column()

    def segment(step, k):
        for r in range(wide):
            lanes = slice(r * LANES, (r + 1) * LANES)
            value = held[k, :, lanes]
            rough = (value * column16[...]).reshape(rows // 16, 16, LANES)
            top = jnp.max(jnp.max(rough, axis=0).astype(jnp.float32), axis=0, keepdims=True)
            value = value.astype(jnp.float32)
            scaled = jnp.exp2(value * column[...] - top)
            weighted[k, :, lanes] = scaled * value
            tops[k, r : r + 1, :] = top
            mine[step, k, r : r + 1, :] = (
                top + jnp.log(jnp.sum(scaled, axis=0, keepdims=True)) * LOG2E
            )

    def send_segments(step, t0):
        for g in range(batch):
            k = lax.rem(base + 1 + t0 + g, owners)
            if g < batch - 1:
                part_copy(step, k, adv, k * stride).start()
            else:
                pl.when(k * stride != adv)(part_copy(step, k, adv, k * stride).start)

    def compute_segments(step, t0):
        for g in range(batch):
            k = lax.rem(base + 1 + t0 + g, owners)
            if step == 0:
                load(k).wait()
            segment(step, k)

    for step in range(ROUNDS):
        compute_segments(step, 0)
        if step == 0:
            pl.semaphore_wait(barrier, n - 1 + m - 1)
        send_segments(step, 0)

        @pl.loop(batch, owners, step=batch)
        def _(t0):
            compute_segments(step, t0)
            send_segments(step, t0)

        def own():
            parts[step, adv] = mine[step, base]
            blocks = parts.at[step, pl.ds(0, n - 1)]
            pltpu.make_async_copy(blocks, blocks, recv_part.at[step]).wait()
            every = parts[step]
            floor = reserve[base] * SCALE
            upper = jnp.maximum(jnp.max(every, axis=0), floor)
            whole = jnp.sum(jnp.exp2(every - upper[None]), axis=0) + jnp.exp2(floor - upper)
            lses[step, base] = upper + jnp.log(whole) * LOG2E

            @pl.loop(1, n, unroll=True)
            def _(t):
                lse_copy(step, base, lax.rem(adv + t, n)).start()

        if_owner(own)
        drain(mine.at[step], send_part.at[step], owners)
        drain(lses.at[step], recv_lse.at[step], owners)
        shares[...] = jnp.exp2(tops[...] - lses[step])

        def gather(b, total):
            for g in range(batch):
                k = b * batch + g
                for r in range(wide):
                    total = total + weighted[k, :, r * LANES : (r + 1) * LANES] * shares[k, r : r + 1, :]
            return total

        total = lax.fori_loop(0, owners // batch, gather, jnp.zeros((rows, LANES), jnp.float32))
        for h in range(halves):
            spends[step, imp, h : h + 1, :] = jnp.sum(
                total[h * LANES : (h + 1) * LANES, :].T, axis=0, keepdims=True
            )

        @pl.loop(1, m)
        def _(t):
            spend_copy(step, imp, lax.rem(imp + t, m)).start()

        if step == ROUNDS - 1:
            price_out[...] = lses[step] * (EPS * LN2)

        def sent():
            blocks = parts.at[step, pl.ds(0, n - 1)]
            pltpu.make_async_copy(blocks, blocks, send_lse.at[step]).wait()

        if_owner(sent)

        @pl.loop(1, m)
        def _(t):
            spend_copy(step, lax.rem(imp + t, m), imp).wait_recv()

        spend = pace_row[...] * jnp.sum(spends[step], axis=0)
        pace_row[...] = jnp.minimum(1.0, pace_row[...] * jnp.sqrt(limits[...] / spend))
        if step < ROUNDS - 1:
            set_column()

        @pl.loop(1, m)
        def _(t):
            spend_copy(step, imp, lax.rem(imp + t, m)).wait_send()

    pace_out[...] = pace_row[...]


def hand_over(pace, prices, pace_out, price_out, sem):
    copies = [
        pltpu.make_async_copy(prices, price_out, sem.at[0]),
        pltpu.make_async_copy(pace, pace_out, sem.at[1]),
    ]
    for copy in copies:
        copy.start()
    for copy in copies:
        copy.wait()


def on_device(n, m, values, limits, start_pace, reserve):
    rows, columns = values.shape
    tiles = columns // LANES
    owners = math.gcd(n, tiles)
    wide = tiles // owners
    halves = rows // LANES
    vmem = pl.BlockSpec(memory_space=pltpu.VMEM)
    f32 = jnp.float32
    pace, prices = pl.pallas_call(
        functools.partial(kernel, n, m, owners),
        out_shape=(
            jax.ShapeDtypeStruct((halves, LANES), f32),
            jax.ShapeDtypeStruct((owners, wide, LANES), f32),
        ),
        in_specs=[pl.BlockSpec(memory_space=pl.ANY), vmem, vmem, vmem],
        out_specs=(vmem, vmem),
        scratch_shapes=[
            pltpu.VMEM((owners, rows, wide * LANES), jnp.bfloat16),
            pltpu.VMEM((owners, rows, wide * LANES), f32),
            pltpu.VMEM((rows, LANES), f32),
            pltpu.VMEM((rows, LANES), jnp.bfloat16),
            pltpu.VMEM((halves, LANES), f32),
            pltpu.VMEM((owners, wide, LANES), f32),
            pltpu.VMEM((owners, wide, LANES), f32),
            pltpu.VMEM((ROUNDS, owners, wide, LANES), f32),
            pltpu.VMEM((ROUNDS, n, wide, LANES), f32),
            pltpu.VMEM((ROUNDS, owners, wide, LANES), f32),
            pltpu.VMEM((ROUNDS, m, halves, LANES), f32),
            pltpu.SemaphoreType.DMA((owners,)),
            pltpu.SemaphoreType.DMA((ROUNDS,)),
            pltpu.SemaphoreType.DMA((ROUNDS,)),
            pltpu.SemaphoreType.DMA((ROUNDS,)),
            pltpu.SemaphoreType.DMA((ROUNDS,)),
            pltpu.SemaphoreType.DMA((ROUNDS, m)),
            pltpu.SemaphoreType.DMA((ROUNDS, m)),
        ],
        compiler_params=pltpu.CompilerParams(
            collective_id=0, has_side_effects=True, vmem_limit_bytes=62 * 2**20
        ),
        name="pacing",
    )(
        values,
        limits.reshape(halves, LANES),
        start_pace.reshape(halves, LANES),
        reserve.reshape(owners, wide, LANES),
    )
    away = pl.BlockSpec(memory_space=pl.ANY)
    pace, prices = pl.pallas_call(
        hand_over,
        out_shape=(
            jax.ShapeDtypeStruct(pace.shape, f32),
            jax.ShapeDtypeStruct(prices.shape, f32),
        ),
        in_specs=[away, away],
        out_specs=(away, away),
        scratch_shapes=[pltpu.SemaphoreType.DMA((2,))],
        compiler_params=pltpu.CompilerParams(vmem_limit_bytes=62 * 2**20),
        name="hand_over",
    )(pace, prices)
    return pace.reshape(rows), prices.reshape(columns)


def solution(mesh):
    placed = (P("adv", "imp"), P("adv"), P("adv"), P("imp"))
    body = functools.partial(on_device, mesh.shape["adv"], mesh.shape["imp"])
    return jax.shard_map(
        body, mesh=mesh, in_specs=placed, out_specs=(P("adv"), P("imp")), check_vma=False
    )
```

```python
import functools
import math

import jax
import jax.numpy as jnp
from jax import lax
from jax.experimental import pallas as pl
from jax.experimental.pallas import tpu as pltpu
from jax.sharding import PartitionSpec as P

ROUNDS = 2
EPS = 0.015
LANES = 128
BATCH = 4
LOG2E = math.log2(math.e)
LN2 = math.log(2.0)
SCALE = LOG2E / EPS


def kernel(
    n, m, owners,
    values, limits, start, reserve,
    pace_out, price_out,
    held, weighted, column, column16, pace_row, limit_row, floors, tops, shares, mine, parts, lses, spends,
    small_sem, load_sem, send_part, recv_part, send_lse, recv_lse, send_spend, recv_spend,
):
    adv, imp = lax.axis_index("adv"), lax.axis_index("imp")
    stride = n // owners
    base = adv // stride
    segs, rows, width = held.shape
    wide = width // LANES
    halves = rows // LANES

    def load(k):
        return pltpu.make_async_copy(
            values.at[:, pl.ds(pl.multiple_of(k * width, width), width)], held.at[k], load_sem.at[k]
        )

    def part_copy(step, k, source, target):
        return pltpu.make_async_remote_copy(
            src_ref=mine.at[step, k], dst_ref=parts.at[step, source],
            send_sem=send_part.at[step], recv_sem=recv_part.at[step],
            device_id=(target, imp), device_id_type=pl.DeviceIdType.MESH,
        )

    def lse_copy(step, k, target):
        return pltpu.make_async_remote_copy(
            src_ref=lses.at[step, k], dst_ref=lses.at[step, k],
            send_sem=send_lse.at[step], recv_sem=recv_lse.at[step, k // batch],
            device_id=(target, imp), device_id_type=pl.DeviceIdType.MESH,
        )

    def spend_copy(step, source, target):
        return pltpu.make_async_remote_copy(
            src_ref=spends.at[step, source], dst_ref=spends.at[step, source],
            send_sem=send_spend.at[step, target], recv_sem=recv_spend.at[step, source],
            device_id=(adv, target), device_id_type=pl.DeviceIdType.MESH,
        )

    is_owner = base * stride == adv
    batch = math.gcd(owners, BATCH)

    def partner(own, c, size):
        if size & (size - 1):
            return lax.rem(own + c, size)
        bits = [1 << i for i in range(size.bit_length() - 1)]
        return sum((lax.rem(own // bit + c // bit, 2) * bit for bit in bits), 0)

    def nearest_last(t):
        return partner(base, owners - 1 - t, owners)

    def drain(ref, sem, most):
        def wait(count):
            blocks = ref.at[pl.ds(0, count)]
            pltpu.make_async_copy(blocks, blocks, sem).wait()

        if stride == 1:
            wait(most - 1)
        else:
            pl.when(is_owner)(lambda: wait(most - 1))
            pl.when(jnp.logical_not(is_owner))(lambda: wait(most))

    def if_owner(run):
        if stride == 1:
            run()
        else:
            pl.when(is_owner)(run)

    barrier = pltpu.get_barrier_semaphore()

    @pl.loop(1, n, unroll=True)
    def _(t):
        pl.semaphore_signal(
            barrier, inc=1, device_id=(lax.rem(adv + t, n), imp), device_id_type=pl.DeviceIdType.MESH
        )

    @pl.loop(1, m, unroll=True)
    def _(t):
        pl.semaphore_signal(
            barrier, inc=1, device_id=(adv, lax.rem(imp + t, m)), device_id_type=pl.DeviceIdType.MESH
        )

    small = [
        pltpu.make_async_copy(source, target, small_sem.at[at])
        for at, (source, target) in enumerate(((start, pace_row), (limits, limit_row), (reserve, floors)))
    ]
    small[0].start()

    @pl.loop(0, owners)
    def _(t):
        load(nearest_last(t)).start()

    small[1].start()
    small[2].start()

    def set_column():
        for h in range(halves):
            spread = jnp.broadcast_to(pace_row[h : h + 1, :], (LANES, LANES)).T * SCALE
            column[h * LANES : (h + 1) * LANES, :] = spread
            column16[h * LANES : (h + 1) * LANES, :] = spread.astype(jnp.bfloat16)

    small[0].wait()
    set_column()

    def segment(step, k):
        for r in range(wide):
            lanes = slice(r * LANES, (r + 1) * LANES)
            value = held[k, :, lanes]
            rough = (value * column16[...]).reshape(rows // 16, 16, LANES)
            top = jnp.max(jnp.max(rough, axis=0).astype(jnp.float32), axis=0, keepdims=True)
            value = value.astype(jnp.float32)
            scaled = jnp.exp2(value * column[...] - top)
            weighted[k, :, lanes] = scaled * value
            tops[k, r : r + 1, :] = top
            mine[step, k, r : r + 1, :] = (
                top + jnp.log(jnp.sum(scaled, axis=0, keepdims=True)) * LOG2E
            )

    def send_segments(step, t0):
        for g in range(batch):
            k = nearest_last(t0 + g)
            if g < batch - 1:
                part_copy(step, k, adv, k * stride).start()
            else:
                pl.when(k * stride != adv)(part_copy(step, k, adv, k * stride).start)

    def compute_segments(step, t0):
        for g in range(batch):
            k = nearest_last(t0 + g)
            if step == 0:
                load(k).wait()
            segment(step, k)

    for step in range(ROUNDS):
        compute_segments(step, 0)
        if step == 0:
            pl.semaphore_wait(barrier, n - 1 + m - 1)
        send_segments(step, 0)

        @pl.loop(batch, owners, step=batch)
        def _(t0):
            compute_segments(step, t0)
            send_segments(step, t0)

        if step == 0:
            small[1].wait()
            small[2].wait()

        def own():
            parts[step, adv] = mine[step, base]
            blocks = parts.at[step, pl.ds(0, n - 1)]
            pltpu.make_async_copy(blocks, blocks, recv_part.at[step]).wait()
            every = parts[step]
            floor = floors[base] * SCALE
            upper = jnp.maximum(jnp.max(every, axis=0), floor)
            whole = jnp.sum(jnp.exp2(every - upper[None]), axis=0) + jnp.exp2(floor - upper)
            lses[step, base] = upper + jnp.log(whole) * LOG2E

            @pl.loop(1, n, unroll=True)
            def _(t):
                lse_copy(step, base, partner(adv, n - t, n)).start()

        if_owner(own)
        drain(mine.at[step], send_part.at[step], owners)
        groups = owners // batch

        def gather(c, total):
            group = partner(base // batch, c, groups)
            first = group * batch
            if isinstance(c, int):
                drain(lses.at[step], recv_lse.at[step, group], batch)
            else:
                blocks = lses.at[step, pl.ds(0, batch)]
                pltpu.make_async_copy(blocks, blocks, recv_lse.at[step, group]).wait()
            members = pl.ds(first, batch)
            shares[...] = jnp.exp2(tops[members] - lses[step, members])
            for g in range(batch):
                for r in range(wide):
                    total = total + (
                        weighted[first + g, :, r * LANES : (r + 1) * LANES] * shares[g, r : r + 1, :]
                    )
            return total

        total = gather(0, jnp.zeros((rows, LANES), jnp.float32))
        total = lax.fori_loop(1, groups, gather, total)
        for h in range(halves):
            spends[step, imp, h : h + 1, :] = jnp.sum(
                total[h * LANES : (h + 1) * LANES, :].T, axis=0, keepdims=True
            )

        @pl.loop(1, m)
        def _(t):
            spend_copy(step, imp, lax.rem(imp + t, m)).start()

        if step == ROUNDS - 1:
            price_out[...] = lses[step] * (EPS * LN2)

        def sent():
            blocks = parts.at[step, pl.ds(0, n - 1)]
            pltpu.make_async_copy(blocks, blocks, send_lse.at[step]).wait()

        if_owner(sent)

        @pl.loop(1, m)
        def _(t):
            spend_copy(step, lax.rem(imp + t, m), imp).wait_recv()

        spend = pace_row[...] * jnp.sum(spends[step], axis=0)
        pace_row[...] = jnp.minimum(1.0, pace_row[...] * jnp.sqrt(limit_row[...] / spend))
        if step < ROUNDS - 1:
            set_column()

        @pl.loop(1, m)
        def _(t):
            spend_copy(step, imp, lax.rem(imp + t, m)).wait_send()

    pace_out[...] = pace_row[...]


def hand_over(pace, prices, pace_out, price_out, sem):
    copies = [
        pltpu.make_async_copy(prices, price_out, sem.at[0]),
        pltpu.make_async_copy(pace, pace_out, sem.at[1]),
    ]
    for copy in copies:
        copy.start()
    for copy in copies:
        copy.wait()


def on_device(n, m, values, limits, start_pace, reserve):
    rows, columns = values.shape
    tiles = columns // LANES
    owners = math.gcd(n, tiles)
    wide = tiles // owners
    halves = rows // LANES
    batch = math.gcd(owners, BATCH)
    vmem = pl.BlockSpec(memory_space=pltpu.VMEM)
    f32 = jnp.float32
    pace, prices = pl.pallas_call(
        functools.partial(kernel, n, m, owners),
        out_shape=(
            jax.ShapeDtypeStruct((halves, LANES), f32),
            jax.ShapeDtypeStruct((owners, wide, LANES), f32),
        ),
        in_specs=[pl.BlockSpec(memory_space=pltpu.HBM)] * 4,
        out_specs=(vmem, vmem),
        scratch_shapes=[
            pltpu.VMEM((owners, rows, wide * LANES), jnp.bfloat16),
            pltpu.VMEM((owners, rows, wide * LANES), f32),
            pltpu.VMEM((rows, LANES), f32),
            pltpu.VMEM((rows, LANES), jnp.bfloat16),
            pltpu.VMEM((halves, LANES), f32),
            pltpu.VMEM((halves, LANES), f32),
            pltpu.VMEM((owners, wide, LANES), f32),
            pltpu.VMEM((owners, wide, LANES), f32),
            pltpu.VMEM((batch, wide, LANES), f32),
            pltpu.VMEM((ROUNDS, owners, wide, LANES), f32),
            pltpu.VMEM((ROUNDS, n, wide, LANES), f32),
            pltpu.VMEM((ROUNDS, owners, wide, LANES), f32),
            pltpu.VMEM((ROUNDS, m, halves, LANES), f32),
            pltpu.SemaphoreType.DMA((3,)),
            pltpu.SemaphoreType.DMA((owners,)),
            pltpu.SemaphoreType.DMA((ROUNDS,)),
            pltpu.SemaphoreType.DMA((ROUNDS,)),
            pltpu.SemaphoreType.DMA((ROUNDS,)),
            pltpu.SemaphoreType.DMA((ROUNDS, owners // batch)),
            pltpu.SemaphoreType.DMA((ROUNDS, m)),
            pltpu.SemaphoreType.DMA((ROUNDS, m)),
        ],
        compiler_params=pltpu.CompilerParams(
            collective_id=0, has_side_effects=True, vmem_limit_bytes=52 * 2**20
        ),
        name="pacing",
    )(
        values,
        limits.reshape(halves, LANES),
        start_pace.reshape(halves, LANES),
        reserve.reshape(owners, wide, LANES),
    )
    away = pl.BlockSpec(memory_space=pl.ANY)
    pace, prices = pl.pallas_call(
        hand_over,
        out_shape=(
            jax.ShapeDtypeStruct(pace.shape, f32),
            jax.ShapeDtypeStruct(prices.shape, f32),
        ),
        in_specs=[away, away],
        out_specs=(away, away),
        scratch_shapes=[pltpu.SemaphoreType.DMA((2,))],
        name="hand_over",
    )(pace, prices)
    return pace.reshape(rows), prices.reshape(columns)


def solution(mesh):
    placed = (P("adv", "imp"), P("adv"), P("adv"), P("imp"))
    body = functools.partial(on_device, mesh.shape["adv"], mesh.shape["imp"])
    return jax.shard_map(
        body, mesh=mesh, in_specs=placed, out_specs=(P("adv"), P("imp")), check_vma=False
    )
```

```python
import functools
import math

import jax
import jax.numpy as jnp
from jax import lax
from jax.experimental import pallas as pl
from jax.experimental.pallas import tpu as pltpu
from jax.sharding import PartitionSpec as P

ROUNDS = 2
EPS = 0.015
LANES = 128
BATCH = 4
LOG2E = math.log2(math.e)
LN2 = math.log(2.0)
SCALE = LOG2E / EPS


def kernel(
    n, m, owners,
    values, limits, start, reserve,
    pace_out, price_out,
    held, weighted, column, column16, pace_row, limit_row, floors, price_row, tops, shares, mine, parts, lses, spends,
    small_sem, out_sem, load_sem, send_part, recv_part, send_lse, recv_lse, send_spend, recv_spend,
):
    adv, imp = lax.axis_index("adv"), lax.axis_index("imp")
    stride = n // owners
    base = adv // stride
    segs, rows, width = held.shape
    wide = width // LANES
    halves = rows // LANES

    def load(k):
        return pltpu.make_async_copy(
            values.at[:, pl.ds(pl.multiple_of(k * width, width), width)], held.at[k], load_sem.at[k]
        )

    def part_copy(step, k, source, target):
        return pltpu.make_async_remote_copy(
            src_ref=mine.at[step, k], dst_ref=parts.at[step, source],
            send_sem=send_part.at[step], recv_sem=recv_part.at[step],
            device_id=(target, imp), device_id_type=pl.DeviceIdType.MESH,
        )

    def lse_copy(step, k, target):
        return pltpu.make_async_remote_copy(
            src_ref=lses.at[step, k], dst_ref=lses.at[step, k],
            send_sem=send_lse.at[step], recv_sem=recv_lse.at[step, k // batch],
            device_id=(target, imp), device_id_type=pl.DeviceIdType.MESH,
        )

    def spend_copy(step, source, target):
        return pltpu.make_async_remote_copy(
            src_ref=spends.at[step, source], dst_ref=spends.at[step, source],
            send_sem=send_spend.at[step, target], recv_sem=recv_spend.at[step, source],
            device_id=(adv, target), device_id_type=pl.DeviceIdType.MESH,
        )

    is_owner = base * stride == adv
    batch = math.gcd(owners, BATCH)

    def partner(own, c, size):
        if size & (size - 1):
            return lax.rem(own + c, size)
        bits = [1 << i for i in range(size.bit_length() - 1)]
        return sum((lax.rem(own // bit + c // bit, 2) * bit for bit in bits), 0)

    def nearest_last(t):
        return partner(base, owners - 1 - t, owners)

    def drain(ref, sem, most):
        def wait(count):
            blocks = ref.at[pl.ds(0, count)]
            pltpu.make_async_copy(blocks, blocks, sem).wait()

        if stride == 1:
            wait(most - 1)
        else:
            pl.when(is_owner)(lambda: wait(most - 1))
            pl.when(jnp.logical_not(is_owner))(lambda: wait(most))

    def if_owner(run):
        if stride == 1:
            run()
        else:
            pl.when(is_owner)(run)

    small = [
        pltpu.make_async_copy(source, target, small_sem.at[at])
        for at, (source, target) in enumerate(((start, pace_row), (limits, limit_row), (reserve, floors)))
    ]
    small[0].start()

    @pl.loop(0, batch, unroll=True)
    def _(t):
        load(nearest_last(t)).start()

    barrier = pltpu.get_barrier_semaphore()

    @pl.loop(1, n, unroll=True)
    def _(t):
        pl.semaphore_signal(
            barrier, inc=1, device_id=(lax.rem(adv + t, n), imp), device_id_type=pl.DeviceIdType.MESH
        )

    @pl.loop(1, m, unroll=True)
    def _(t):
        pl.semaphore_signal(
            barrier, inc=1, device_id=(adv, lax.rem(imp + t, m)), device_id_type=pl.DeviceIdType.MESH
        )

    @pl.loop(batch, owners, unroll=True)
    def _(t):
        load(nearest_last(t)).start()

    small[1].start()
    small[2].start()

    def set_column():
        for h in range(halves):
            spread = jnp.broadcast_to(pace_row[h : h + 1, :], (LANES, LANES)).T * SCALE
            column[h * LANES : (h + 1) * LANES, :] = spread
            column16[h * LANES : (h + 1) * LANES, :] = spread.astype(jnp.bfloat16)

    small[0].wait()
    set_column()

    def segment(step, k):
        for r in range(wide):
            lanes = slice(r * LANES, (r + 1) * LANES)
            value = held[k, :, lanes]
            rough = (value * column16[...]).reshape(rows // 16, 16, LANES)
            top = jnp.max(jnp.max(rough, axis=0).astype(jnp.float32), axis=0, keepdims=True)
            value = value.astype(jnp.float32)
            scaled = jnp.exp2(value * column[...] - top)
            weighted[k, :, lanes] = scaled * value
            tops[k, r : r + 1, :] = top
            mine[step, k, r : r + 1, :] = (
                top + jnp.log(jnp.sum(scaled, axis=0, keepdims=True)) * LOG2E
            )

    def send_segments(step, t0):
        for g in range(batch):
            k = nearest_last(t0 + g)
            if g < batch - 1:
                part_copy(step, k, adv, k * stride).start()
            else:
                pl.when(k * stride != adv)(part_copy(step, k, adv, k * stride).start)

    def compute_segments(step, t0):
        for g in range(batch):
            k = nearest_last(t0 + g)
            if step == 0:
                load(k).wait()
            segment(step, k)

    for step in range(ROUNDS):
        compute_segments(step, 0)
        if step == 0:
            pl.semaphore_wait(barrier, n - 1 + m - 1)
        send_segments(step, 0)

        @pl.loop(batch, owners, step=batch)
        def _(t0):
            compute_segments(step, t0)
            send_segments(step, t0)

        if step == 0:
            small[1].wait()
            small[2].wait()

        def own():
            parts[step, adv] = mine[step, base]
            blocks = parts.at[step, pl.ds(0, n - 1)]
            pltpu.make_async_copy(blocks, blocks, recv_part.at[step]).wait()
            every = parts[step]
            floor = floors[base] * SCALE
            upper = jnp.maximum(jnp.max(every, axis=0), floor)
            whole = jnp.sum(jnp.exp2(every - upper[None]), axis=0) + jnp.exp2(floor - upper)
            lses[step, base] = upper + jnp.log(whole) * LOG2E

            @pl.loop(1, n, unroll=True)
            def _(t):
                lse_copy(step, base, partner(adv, n - t, n)).start()

        if_owner(own)
        drain(mine.at[step], send_part.at[step], owners)
        groups = owners // batch

        def gather(c, total):
            group = partner(base // batch, c, groups)
            first = group * batch
            if isinstance(c, int):
                drain(lses.at[step], recv_lse.at[step, group], batch)
            else:
                blocks = lses.at[step, pl.ds(0, batch)]
                pltpu.make_async_copy(blocks, blocks, recv_lse.at[step, group]).wait()
            members = pl.ds(first, batch)
            shares[...] = jnp.exp2(tops[members] - lses[step, members])
            for g in range(batch):
                for r in range(wide):
                    total = total + (
                        weighted[first + g, :, r * LANES : (r + 1) * LANES] * shares[g, r : r + 1, :]
                    )
            return total

        total = gather(0, jnp.zeros((rows, LANES), jnp.float32))
        total = lax.fori_loop(1, groups, gather, total)
        for h in range(halves):
            spends[step, imp, h : h + 1, :] = jnp.sum(
                total[h * LANES : (h + 1) * LANES, :].T, axis=0, keepdims=True
            )

        @pl.loop(1, m)
        def _(t):
            spend_copy(step, imp, lax.rem(imp + t, m)).start()

        if step == ROUNDS - 1:
            price_row[...] = lses[step] * (EPS * LN2)
            price_copy = pltpu.make_async_copy(price_row, price_out, out_sem.at[0])
            price_copy.start()

        def sent():
            blocks = parts.at[step, pl.ds(0, n - 1)]
            pltpu.make_async_copy(blocks, blocks, send_lse.at[step]).wait()

        if_owner(sent)

        @pl.loop(1, m)
        def _(t):
            spend_copy(step, lax.rem(imp + t, m), imp).wait_recv()

        spend = pace_row[...] * jnp.sum(spends[step], axis=0)
        pace_row[...] = jnp.minimum(1.0, pace_row[...] * jnp.sqrt(limit_row[...] / spend))
        if step < ROUNDS - 1:
            set_column()

    pace_copy = pltpu.make_async_copy(pace_row, pace_out, out_sem.at[1])
    pace_copy.start()
    for step in range(ROUNDS):

        @pl.loop(1, m)
        def _(t):
            spend_copy(step, imp, lax.rem(imp + t, m)).wait_send()

    price_copy.wait()
    pace_copy.wait()


def hand_over(pace, prices, pace_out, price_out):
    pace_out[...] = pace[...]
    price_out[...] = prices[...]


def on_device(n, m, values, limits, start_pace, reserve):
    rows, columns = values.shape
    tiles = columns // LANES
    owners = math.gcd(n, tiles)
    wide = tiles // owners
    halves = rows // LANES
    batch = math.gcd(owners, BATCH)
    vmem = pl.BlockSpec(memory_space=pltpu.VMEM)
    away = pl.BlockSpec(memory_space=pltpu.HBM)
    f32 = jnp.float32
    pace, prices = pl.pallas_call(
        functools.partial(kernel, n, m, owners),
        out_shape=(
            jax.ShapeDtypeStruct((halves, LANES), f32),
            jax.ShapeDtypeStruct((owners, wide, LANES), f32),
        ),
        in_specs=[away] * 4,
        out_specs=(away, away),
        scratch_shapes=[
            pltpu.VMEM((owners, rows, wide * LANES), jnp.bfloat16),
            pltpu.VMEM((owners, rows, wide * LANES), f32),
            pltpu.VMEM((rows, LANES), f32),
            pltpu.VMEM((rows, LANES), jnp.bfloat16),
            pltpu.VMEM((halves, LANES), f32),
            pltpu.VMEM((halves, LANES), f32),
            pltpu.VMEM((owners, wide, LANES), f32),
            pltpu.VMEM((owners, wide, LANES), f32),
            pltpu.VMEM((owners, wide, LANES), f32),
            pltpu.VMEM((batch, wide, LANES), f32),
            pltpu.VMEM((ROUNDS, owners, wide, LANES), f32),
            pltpu.VMEM((ROUNDS, n, wide, LANES), f32),
            pltpu.VMEM((ROUNDS, owners, wide, LANES), f32),
            pltpu.VMEM((ROUNDS, m, halves, LANES), f32),
            pltpu.SemaphoreType.DMA((3,)),
            pltpu.SemaphoreType.DMA((2,)),
            pltpu.SemaphoreType.DMA((owners,)),
            pltpu.SemaphoreType.DMA((ROUNDS,)),
            pltpu.SemaphoreType.DMA((ROUNDS,)),
            pltpu.SemaphoreType.DMA((ROUNDS,)),
            pltpu.SemaphoreType.DMA((ROUNDS, owners // batch)),
            pltpu.SemaphoreType.DMA((ROUNDS, m)),
            pltpu.SemaphoreType.DMA((ROUNDS, m)),
        ],
        compiler_params=pltpu.CompilerParams(
            collective_id=0, has_side_effects=True, vmem_limit_bytes=62 * 2**20
        ),
        name="pacing",
    )(
        values,
        limits.reshape(halves, LANES),
        start_pace.reshape(halves, LANES),
        reserve.reshape(owners, wide, LANES),
    )
    pace, prices = pl.pallas_call(
        hand_over,
        out_shape=(
            jax.ShapeDtypeStruct(pace.shape, f32),
            jax.ShapeDtypeStruct(prices.shape, f32),
        ),
        in_specs=[vmem, vmem],
        out_specs=(vmem, vmem),
        compiler_params=pltpu.CompilerParams(vmem_limit_bytes=62 * 2**20),
        name="hand_over",
    )(pace, prices)
    return pace.reshape(rows), prices.reshape(columns)


def solution(mesh):
    placed = (P("adv", "imp"), P("adv"), P("adv"), P("imp"))
    body = functools.partial(on_device, mesh.shape["adv"], mesh.shape["imp"])
    return jax.shard_map(
        body, mesh=mesh, in_specs=placed, out_specs=(P("adv"), P("imp")), check_vma=False
    )
```

```python
import functools
import math

import jax
import jax.numpy as jnp
from jax import lax
from jax.experimental import pallas as pl
from jax.experimental.pallas import tpu as pltpu
from jax.sharding import PartitionSpec as P

ROUNDS = 2
EPS = 0.015
LANES = 128
BATCH = 4
LOG2E = math.log2(math.e)
LN2 = math.log(2.0)
SCALE = LOG2E / EPS


def kernel(
    n, m, owners,
    values, limits, start, reserve,
    pace_out, price_out,
    held, weighted, column, column16, pace_row, limit_row, floors, price_row, tops, shares, mine, parts, lses, spends,
    small_sem, out_sem, load_sem, send_part, recv_part, send_lse, recv_lse, send_spend, recv_spend,
):
    adv, imp = lax.axis_index("adv"), lax.axis_index("imp")
    stride = n // owners
    base = adv // stride
    segs, rows, width = held.shape
    wide = width // LANES
    halves = rows // LANES
    batch = math.gcd(owners, BATCH)

    def load(k):
        return pltpu.make_async_copy(
            values.at[:, pl.ds(pl.multiple_of(k * width, width), width)], held.at[k], load_sem.at[k]
        )

    def part_copy(step, k, source, target):
        return pltpu.make_async_remote_copy(
            src_ref=mine.at[step, k], dst_ref=parts.at[step, source],
            send_sem=send_part.at[step], recv_sem=recv_part.at[step],
            device_id=(target, imp), device_id_type=pl.DeviceIdType.MESH,
        )

    def lse_copy(step, k, target):
        return pltpu.make_async_remote_copy(
            src_ref=lses.at[step, k], dst_ref=lses.at[step, k],
            send_sem=send_lse.at[step], recv_sem=recv_lse.at[step, k // batch],
            device_id=(target, imp), device_id_type=pl.DeviceIdType.MESH,
        )

    def spend_copy(step, source, target):
        return pltpu.make_async_remote_copy(
            src_ref=spends.at[step, source], dst_ref=spends.at[step, source],
            send_sem=send_spend.at[step, target], recv_sem=recv_spend.at[step, source],
            device_id=(adv, target), device_id_type=pl.DeviceIdType.MESH,
        )

    is_owner = base * stride == adv

    def bit_steps(own, size):
        return [(1 - 2 * lax.rem(lax.div(own, 1 << i), 2)) << i for i in range(size.bit_length() - 1)]

    def partner(own, steps, c, size):
        if size & (size - 1):
            return lax.rem(own + c, size)
        if isinstance(c, int):
            return own + sum((step for i, step in enumerate(steps) if c >> i & 1), 0)
        return own + sum((step * lax.rem(lax.div(c, 1 << i), 2) for i, step in enumerate(steps)), 0)

    groups = owners // batch
    home, seat = lax.div(base, batch), lax.rem(base, batch)
    home_steps, seat_steps = bit_steps(home, groups), bit_steps(seat, batch)
    adv_steps = bit_steps(adv, n)

    def members(b):
        first = partner(home, home_steps, groups - 1 - b, groups) * batch
        return [first + partner(seat, seat_steps, batch - 1 - g, batch) for g in range(batch)]

    def drain(ref, sem, most):
        def wait(count):
            blocks = ref.at[pl.ds(0, count)]
            pltpu.make_async_copy(blocks, blocks, sem).wait()

        if stride == 1:
            wait(most - 1)
        else:
            pl.when(is_owner)(lambda: wait(most - 1))
            pl.when(jnp.logical_not(is_owner))(lambda: wait(most))

    def if_owner(run):
        if stride == 1:
            run()
        else:
            pl.when(is_owner)(run)

    small = [
        pltpu.make_async_copy(source, target, small_sem.at[at])
        for at, (source, target) in enumerate(((start, pace_row), (limits, limit_row), (reserve, floors)))
    ]
    small[0].start()

    for k in members(0):
        load(k).start()

    barrier = pltpu.get_barrier_semaphore()

    @pl.loop(1, n, unroll=True)
    def _(t):
        pl.semaphore_signal(
            barrier, inc=1, device_id=(lax.rem(adv + t, n), imp), device_id_type=pl.DeviceIdType.MESH
        )

    @pl.loop(1, m, unroll=True)
    def _(t):
        pl.semaphore_signal(
            barrier, inc=1, device_id=(adv, lax.rem(imp + t, m)), device_id_type=pl.DeviceIdType.MESH
        )

    @pl.loop(1, groups)
    def _(b):
        for k in members(b):
            load(k).start()

    small[1].start()
    small[2].start()

    def set_column():
        for h in range(halves):
            spread = jnp.broadcast_to(pace_row[h : h + 1, :], (LANES, LANES)).T * SCALE
            column[h * LANES : (h + 1) * LANES, :] = spread
            column16[h * LANES : (h + 1) * LANES, :] = spread.astype(jnp.bfloat16)

    small[0].wait()
    set_column()

    price_copy = pltpu.make_async_copy(price_row, price_out, out_sem.at[0])

    def segment(step, k):
        for r in range(wide):
            lanes = slice(r * LANES, (r + 1) * LANES)
            value = held[k, :, lanes]
            rough = (value * column16[...]).reshape(rows // 16, 16, LANES)
            top = jnp.max(jnp.max(rough, axis=0).astype(jnp.float32), axis=0, keepdims=True)
            value = value.astype(jnp.float32)
            scaled = jnp.exp2(value * column[...] - top)
            weighted[k, :, lanes] = scaled * value
            tops[k, r : r + 1, :] = top
            mine[step, k, r : r + 1, :] = (
                top + jnp.log(jnp.sum(scaled, axis=0, keepdims=True)) * LOG2E
            )

    @pl.loop(0, ROUNDS)
    def _(step):
        @pl.loop(0, groups)
        def _(b):
            ks = members(b)

            @pl.when(step == 0)
            def _():
                for k in ks:
                    load(k).wait()

            for k in ks:
                segment(step, k)

            @pl.when(jnp.logical_and(step == 0, b == 0))
            def _():
                pl.semaphore_wait(barrier, n - 1 + m - 1)

            for k in ks[:-1]:
                part_copy(step, k, adv, k * stride).start()
            pl.when(ks[-1] * stride != adv)(part_copy(step, ks[-1], adv, ks[-1] * stride).start)

        @pl.when(step == 0)
        def _():
            small[1].wait()
            small[2].wait()

        def own():
            parts[step, adv] = mine[step, base]
            blocks = parts.at[step, pl.ds(0, n - 1)]
            pltpu.make_async_copy(blocks, blocks, recv_part.at[step]).wait()
            every = parts[step]
            floor = floors[base] * SCALE
            upper = jnp.maximum(jnp.max(every, axis=0), floor)
            whole = jnp.sum(jnp.exp2(every - upper[None]), axis=0) + jnp.exp2(floor - upper)
            lses[step, base] = upper + jnp.log(whole) * LOG2E

            for c in range(n - 1, 0, -1):
                lse_copy(step, base, partner(adv, adv_steps, c, n)).start()

        if_owner(own)
        drain(mine.at[step], send_part.at[step], owners)
        def gather(c, total):
            group = partner(home, home_steps, c, groups)
            first = group * batch

            @pl.when(c == 0)
            def _():
                drain(lses.at[step], recv_lse.at[step, group], batch)

            @pl.when(c > 0)
            def _():
                blocks = lses.at[step, pl.ds(0, batch)]
                pltpu.make_async_copy(blocks, blocks, recv_lse.at[step, group]).wait()

            here = pl.ds(first, batch)
            shares[...] = jnp.exp2(tops[here] - lses[step, here])
            for g in range(batch):
                for r in range(wide):
                    total = total + (
                        weighted[first + g, :, r * LANES : (r + 1) * LANES] * shares[g, r : r + 1, :]
                    )
            return total

        total = lax.fori_loop(0, groups, gather, jnp.zeros((rows, LANES), jnp.float32))
        for h in range(halves):
            spends[step, imp, h : h + 1, :] = jnp.sum(
                total[h * LANES : (h + 1) * LANES, :].T, axis=0, keepdims=True
            )

        @pl.loop(1, m)
        def _(t):
            spend_copy(step, imp, lax.rem(imp + t, m)).start()

        @pl.when(step == ROUNDS - 1)
        def _():
            price_row[...] = lses[step] * (EPS * LN2)
            price_copy.start()

        def sent():
            blocks = parts.at[step, pl.ds(0, n - 1)]
            pltpu.make_async_copy(blocks, blocks, send_lse.at[step]).wait()

        if_owner(sent)

        @pl.loop(1, m)
        def _(t):
            spend_copy(step, lax.rem(imp + t, m), imp).wait_recv()

        spend = pace_row[...] * jnp.sum(spends[step], axis=0)
        pace_row[...] = jnp.minimum(1.0, pace_row[...] * jnp.sqrt(limit_row[...] / spend))
        pl.when(step < ROUNDS - 1)(set_column)

    pace_copy = pltpu.make_async_copy(pace_row, pace_out, out_sem.at[1])
    pace_copy.start()
    for step in range(ROUNDS):

        @pl.loop(1, m)
        def _(t):
            spend_copy(step, imp, lax.rem(imp + t, m)).wait_send()

    price_copy.wait()
    pace_copy.wait()


def hand_over(pace, prices, pace_out, price_out):
    pace_out[...] = pace[...]
    price_out[...] = prices[...]


def on_device(n, m, values, limits, start_pace, reserve):
    rows, columns = values.shape
    tiles = columns // LANES
    owners = math.gcd(n, tiles)
    wide = tiles // owners
    halves = rows // LANES
    batch = math.gcd(owners, BATCH)
    vmem = pl.BlockSpec(memory_space=pltpu.VMEM)
    away = pl.BlockSpec(memory_space=pltpu.HBM)
    f32 = jnp.float32
    pace, prices = pl.pallas_call(
        functools.partial(kernel, n, m, owners),
        out_shape=(
            jax.ShapeDtypeStruct((halves, LANES), f32),
            jax.ShapeDtypeStruct((owners, wide, LANES), f32),
        ),
        in_specs=[away] * 4,
        out_specs=(away, away),
        scratch_shapes=[
            pltpu.VMEM((owners, rows, wide * LANES), jnp.bfloat16),
            pltpu.VMEM((owners, rows, wide * LANES), f32),
            pltpu.VMEM((rows, LANES), f32),
            pltpu.VMEM((rows, LANES), jnp.bfloat16),
            pltpu.VMEM((halves, LANES), f32),
            pltpu.VMEM((halves, LANES), f32),
            pltpu.VMEM((owners, wide, LANES), f32),
            pltpu.VMEM((owners, wide, LANES), f32),
            pltpu.VMEM((owners, wide, LANES), f32),
            pltpu.VMEM((batch, wide, LANES), f32),
            pltpu.VMEM((ROUNDS, owners, wide, LANES), f32),
            pltpu.VMEM((ROUNDS, n, wide, LANES), f32),
            pltpu.VMEM((ROUNDS, owners, wide, LANES), f32),
            pltpu.VMEM((ROUNDS, m, halves, LANES), f32),
            pltpu.SemaphoreType.DMA((3,)),
            pltpu.SemaphoreType.DMA((2,)),
            pltpu.SemaphoreType.DMA((owners,)),
            pltpu.SemaphoreType.DMA((ROUNDS,)),
            pltpu.SemaphoreType.DMA((ROUNDS,)),
            pltpu.SemaphoreType.DMA((ROUNDS,)),
            pltpu.SemaphoreType.DMA((ROUNDS, owners // batch)),
            pltpu.SemaphoreType.DMA((ROUNDS, m)),
            pltpu.SemaphoreType.DMA((ROUNDS, m)),
        ],
        compiler_params=pltpu.CompilerParams(
            collective_id=0, has_side_effects=True, vmem_limit_bytes=62 * 2**20
        ),
        name="pacing",
    )(
        values,
        limits.reshape(halves, LANES),
        start_pace.reshape(halves, LANES),
        reserve.reshape(owners, wide, LANES),
    )
    pace, prices = pl.pallas_call(
        hand_over,
        out_shape=(
            jax.ShapeDtypeStruct(pace.shape, f32),
            jax.ShapeDtypeStruct(prices.shape, f32),
        ),
        in_specs=[vmem, vmem],
        out_specs=(vmem, vmem),
        compiler_params=pltpu.CompilerParams(vmem_limit_bytes=62 * 2**20),
        name="hand_over",
    )(pace, prices)
    return pace.reshape(rows), prices.reshape(columns)


def solution(mesh):
    placed = (P("adv", "imp"), P("adv"), P("adv"), P("imp"))
    body = functools.partial(on_device, mesh.shape["adv"], mesh.shape["imp"])
    return jax.shard_map(
        body, mesh=mesh, in_specs=placed, out_specs=(P("adv"), P("imp")), check_vma=False
    )
```

```python
import functools
import math

import jax
import jax.numpy as jnp
from jax import lax
from jax.experimental import pallas as pl
from jax.experimental.pallas import tpu as pltpu
from jax.sharding import PartitionSpec as P

ROUNDS = 2
EPS = 0.015
LANES = 128
BATCH = 4
TALL = 64
LOG2E = math.log2(math.e)
LN2 = math.log(2.0)
SCALE = LOG2E / EPS


def kernel(
    n, m, owners,
    values, limits, start, reserve,
    pace_out, price_out,
    held, weighted, column, column16, pace_row, limit_row, floors, price_row, tops, shares, mine, parts, lses, spends,
    small_sem, out_sem, load_sem, send_part, recv_part, send_lse, recv_lse, send_spend, recv_spend,
):
    adv, imp = lax.axis_index("adv"), lax.axis_index("imp")
    stride = n // owners
    base = adv // stride
    segs, rows, width = held.shape
    wide = width // LANES
    halves = rows // LANES
    batch = math.gcd(owners, BATCH)

    def load(k):
        return pltpu.make_async_copy(
            values.at[:, pl.ds(pl.multiple_of(k * width, width), width)], held.at[k], load_sem.at[k]
        )

    def part_copy(step, k, source, target):
        return pltpu.make_async_remote_copy(
            src_ref=mine.at[step, k], dst_ref=parts.at[step, source],
            send_sem=send_part.at[step], recv_sem=recv_part.at[step],
            device_id=(target, imp), device_id_type=pl.DeviceIdType.MESH,
        )

    def lse_copy(step, k, target):
        return pltpu.make_async_remote_copy(
            src_ref=lses.at[step, k], dst_ref=lses.at[step, k],
            send_sem=send_lse.at[step], recv_sem=recv_lse.at[step, k // batch],
            device_id=(target, imp), device_id_type=pl.DeviceIdType.MESH,
        )

    def spend_copy(step, source, target):
        return pltpu.make_async_remote_copy(
            src_ref=spends.at[step, source], dst_ref=spends.at[step, source],
            send_sem=send_spend.at[step, target], recv_sem=recv_spend.at[step, source],
            device_id=(adv, target), device_id_type=pl.DeviceIdType.MESH,
        )

    is_owner = base * stride == adv

    def bit_steps(own, size):
        return [(1 - 2 * lax.rem(lax.div(own, 1 << i), 2)) << i for i in range(size.bit_length() - 1)]

    def partner(own, steps, c, size):
        if size & (size - 1):
            return lax.rem(own + c, size)
        if isinstance(c, int):
            return own + sum((step for i, step in enumerate(steps) if c >> i & 1), 0)
        return own + sum((step * lax.rem(lax.div(c, 1 << i), 2) for i, step in enumerate(steps)), 0)

    groups = owners // batch
    home, seat = lax.div(base, batch), lax.rem(base, batch)
    home_steps, seat_steps = bit_steps(home, groups), bit_steps(seat, batch)
    adv_steps = bit_steps(adv, n)

    def members(b):
        first = partner(home, home_steps, groups - 1 - b, groups) * batch
        return [first + partner(seat, seat_steps, batch - 1 - g, batch) for g in range(batch)]

    def drain(ref, sem, most):
        def wait(count):
            blocks = ref.at[pl.ds(0, count)]
            pltpu.make_async_copy(blocks, blocks, sem).wait()

        if stride == 1:
            wait(most - 1)
        else:
            pl.when(is_owner)(lambda: wait(most - 1))
            pl.when(jnp.logical_not(is_owner))(lambda: wait(most))

    def if_owner(run):
        if stride == 1:
            run()
        else:
            pl.when(is_owner)(run)

    small = [
        pltpu.make_async_copy(source, target, small_sem.at[at])
        for at, (source, target) in enumerate(((start, pace_row), (limits, limit_row), (reserve, floors)))
    ]
    small[0].start()

    for k in members(0):
        load(k).start()

    barrier = pltpu.get_barrier_semaphore()

    @pl.loop(1, n, unroll=True)
    def _(t):
        pl.semaphore_signal(
            barrier, inc=1, device_id=(lax.rem(adv + t, n), imp), device_id_type=pl.DeviceIdType.MESH
        )

    @pl.loop(1, m, unroll=True)
    def _(t):
        pl.semaphore_signal(
            barrier, inc=1, device_id=(adv, lax.rem(imp + t, m)), device_id_type=pl.DeviceIdType.MESH
        )

    @pl.loop(1, groups)
    def _(b):
        for k in members(b):
            load(k).start()

    small[1].start()
    small[2].start()

    def set_column():
        for h in range(halves):
            spread = jnp.broadcast_to(pace_row[h : h + 1, :], (LANES, LANES)).T * SCALE
            column[h * LANES : (h + 1) * LANES, :] = spread
            column16[h * LANES : (h + 1) * LANES, :] = spread.astype(jnp.bfloat16)

    small[0].wait()
    set_column()

    price_copy = pltpu.make_async_copy(price_row, price_out, out_sem.at[0])

    tall = math.gcd(rows, TALL)
    blocks = [slice(at, at + tall) for at in range(0, rows, tall)]

    def segment(step, k):
        for r in range(wide):
            lanes = slice(r * LANES, (r + 1) * LANES)
            rough = held[k, blocks[0], lanes] * column16[blocks[0], :]
            for block in blocks[1:]:
                rough = jnp.maximum(rough, held[k, block, lanes] * column16[block, :])
            top = jnp.max(rough.astype(jnp.float32), axis=0, keepdims=True)
            tally = jnp.zeros((8, LANES), jnp.float32)
            for block in blocks:
                value = held[k, block, lanes].astype(jnp.float32)
                scaled = jnp.exp2(value * column[block, :] - top)
                weighted[k, block, lanes] = scaled * value
                tally = tally + jnp.sum(scaled.reshape(-1, 8, LANES), axis=0)
            tops[k, r : r + 1, :] = top
            mine[step, k, r : r + 1, :] = (
                top + jnp.log(jnp.sum(tally, axis=0, keepdims=True)) * LOG2E
            )

    @pl.loop(0, ROUNDS)
    def _(step):
        @pl.loop(0, groups)
        def _(b):
            ks = members(b)

            @pl.when(step == 0)
            def _():
                for k in ks:
                    load(k).wait()

            for k in ks:
                segment(step, k)

            @pl.when(jnp.logical_and(step == 0, b == 0))
            def _():
                pl.semaphore_wait(barrier, n - 1 + m - 1)

            for k in ks[:-1]:
                part_copy(step, k, adv, k * stride).start()
            pl.when(ks[-1] * stride != adv)(part_copy(step, ks[-1], adv, ks[-1] * stride).start)

        @pl.when(step == 0)
        def _():
            small[1].wait()
            small[2].wait()

        def own():
            parts[step, adv] = mine[step, base]
            blocks = parts.at[step, pl.ds(0, n - 1)]
            pltpu.make_async_copy(blocks, blocks, recv_part.at[step]).wait()
            every = parts[step]
            floor = floors[base] * SCALE
            upper = jnp.maximum(jnp.max(every, axis=0), floor)
            whole = jnp.sum(jnp.exp2(every - upper[None]), axis=0) + jnp.exp2(floor - upper)
            lses[step, base] = upper + jnp.log(whole) * LOG2E

            for c in range(n - 1, 0, -1):
                lse_copy(step, base, partner(adv, adv_steps, c, n)).start()

        if_owner(own)
        drain(mine.at[step], send_part.at[step], owners)
        def gather(c, total):
            group = partner(home, home_steps, c, groups)
            first = group * batch

            @pl.when(c == 0)
            def _():
                drain(lses.at[step], recv_lse.at[step, group], batch)

            @pl.when(c > 0)
            def _():
                every = lses.at[step, pl.ds(0, batch)]
                pltpu.make_async_copy(every, every, recv_lse.at[step, group]).wait()

            here = pl.ds(first, batch)
            shares[...] = jnp.exp2(tops[here] - lses[step, here])
            sums = []
            for block, part in zip(blocks, total):
                for g in range(batch):
                    for r in range(wide):
                        lanes = slice(r * LANES, (r + 1) * LANES)
                        part = part + weighted[first + g, block, lanes] * shares[g, r : r + 1, :]
                sums.append(part)
            return tuple(sums)

        nothing = jnp.zeros((tall, LANES), jnp.float32)
        total = lax.fori_loop(0, groups, gather, (nothing,) * len(blocks))
        total = jnp.concatenate(total, axis=0)
        for h in range(halves):
            spends[step, imp, h : h + 1, :] = jnp.sum(
                total[h * LANES : (h + 1) * LANES, :].T, axis=0, keepdims=True
            )

        @pl.loop(1, m)
        def _(t):
            spend_copy(step, imp, lax.rem(imp + t, m)).start()

        @pl.when(step == ROUNDS - 1)
        def _():
            price_row[...] = lses[step] * (EPS * LN2)
            price_copy.start()

        def sent():
            blocks = parts.at[step, pl.ds(0, n - 1)]
            pltpu.make_async_copy(blocks, blocks, send_lse.at[step]).wait()

        if_owner(sent)

        @pl.loop(1, m)
        def _(t):
            spend_copy(step, lax.rem(imp + t, m), imp).wait_recv()

        spend = pace_row[...] * jnp.sum(spends[step], axis=0)
        pace_row[...] = jnp.minimum(1.0, pace_row[...] * jnp.sqrt(limit_row[...] / spend))
        pl.when(step < ROUNDS - 1)(set_column)

    pace_copy = pltpu.make_async_copy(pace_row, pace_out, out_sem.at[1])
    pace_copy.start()
    for step in range(ROUNDS):

        @pl.loop(1, m)
        def _(t):
            spend_copy(step, imp, lax.rem(imp + t, m)).wait_send()

    price_copy.wait()
    pace_copy.wait()


def hand_over(pace, prices, pace_out, price_out):
    pace_out[...] = pace[...]
    price_out[...] = prices[...]


def on_device(n, m, values, limits, start_pace, reserve):
    rows, columns = values.shape
    tiles = columns // LANES
    owners = math.gcd(n, tiles)
    wide = tiles // owners
    halves = rows // LANES
    batch = math.gcd(owners, BATCH)
    vmem = pl.BlockSpec(memory_space=pltpu.VMEM)
    away = pl.BlockSpec(memory_space=pltpu.HBM)
    f32 = jnp.float32
    pace, prices = pl.pallas_call(
        functools.partial(kernel, n, m, owners),
        out_shape=(
            jax.ShapeDtypeStruct((halves, LANES), f32),
            jax.ShapeDtypeStruct((owners, wide, LANES), f32),
        ),
        in_specs=[away] * 4,
        out_specs=(away, away),
        scratch_shapes=[
            pltpu.VMEM((owners, rows, wide * LANES), jnp.bfloat16),
            pltpu.VMEM((owners, rows, wide * LANES), f32),
            pltpu.VMEM((rows, LANES), f32),
            pltpu.VMEM((rows, LANES), jnp.bfloat16),
            pltpu.VMEM((halves, LANES), f32),
            pltpu.VMEM((halves, LANES), f32),
            pltpu.VMEM((owners, wide, LANES), f32),
            pltpu.VMEM((owners, wide, LANES), f32),
            pltpu.VMEM((owners, wide, LANES), f32),
            pltpu.VMEM((batch, wide, LANES), f32),
            pltpu.VMEM((ROUNDS, owners, wide, LANES), f32),
            pltpu.VMEM((ROUNDS, n, wide, LANES), f32),
            pltpu.VMEM((ROUNDS, owners, wide, LANES), f32),
            pltpu.VMEM((ROUNDS, m, halves, LANES), f32),
            pltpu.SemaphoreType.DMA((3,)),
            pltpu.SemaphoreType.DMA((2,)),
            pltpu.SemaphoreType.DMA((owners,)),
            pltpu.SemaphoreType.DMA((ROUNDS,)),
            pltpu.SemaphoreType.DMA((ROUNDS,)),
            pltpu.SemaphoreType.DMA((ROUNDS,)),
            pltpu.SemaphoreType.DMA((ROUNDS, owners // batch)),
            pltpu.SemaphoreType.DMA((ROUNDS, m)),
            pltpu.SemaphoreType.DMA((ROUNDS, m)),
        ],
        compiler_params=pltpu.CompilerParams(
            collective_id=0, has_side_effects=True, vmem_limit_bytes=62 * 2**20
        ),
        name="pacing",
    )(
        values,
        limits.reshape(halves, LANES),
        start_pace.reshape(halves, LANES),
        reserve.reshape(owners, wide, LANES),
    )
    pace, prices = pl.pallas_call(
        hand_over,
        out_shape=(
            jax.ShapeDtypeStruct(pace.shape, f32),
            jax.ShapeDtypeStruct(prices.shape, f32),
        ),
        in_specs=[vmem, vmem],
        out_specs=(vmem, vmem),
        compiler_params=pltpu.CompilerParams(vmem_limit_bytes=62 * 2**20),
        name="hand_over",
    )(pace, prices)
    return pace.reshape(rows), prices.reshape(columns)


def solution(mesh):
    placed = (P("adv", "imp"), P("adv"), P("adv"), P("imp"))
    body = functools.partial(on_device, mesh.shape["adv"], mesh.shape["imp"])
    return jax.shard_map(
        body, mesh=mesh, in_specs=placed, out_specs=(P("adv"), P("imp")), check_vma=False
    )
```

```python
import functools
import math

import jax
import jax.numpy as jnp
from jax import lax
from jax.experimental import pallas as pl
from jax.experimental.pallas import tpu as pltpu
from jax.sharding import PartitionSpec as P

ROUNDS = 2
EPS = 0.015
LANES = 128
BATCH = 2
TALL = 64
LOG2E = math.log2(math.e)
LN2 = math.log(2.0)
SCALE = LOG2E / EPS


def kernel(
    n, m, owners,
    values, limits, start, reserve,
    pace_out, price_out,
    held, weighted, column, column16, pace_row, limit_row, floors, price_row, tops, shares, mine, parts, lses, spends,
    small_sem, out_sem, load_sem, send_part, recv_part, send_lse, recv_lse, send_spend, recv_spend,
):
    adv, imp = lax.axis_index("adv"), lax.axis_index("imp")
    stride = n // owners
    base = adv // stride
    segs, rows, width = held.shape
    wide = width // LANES
    halves = rows // LANES
    batch = math.gcd(owners, BATCH)

    def load(k):
        return pltpu.make_async_copy(
            values.at[:, pl.ds(pl.multiple_of(k * width, width), width)], held.at[k], load_sem.at[k]
        )

    def part_copy(step, k, source, target):
        return pltpu.make_async_remote_copy(
            src_ref=mine.at[step, k], dst_ref=parts.at[step, source],
            send_sem=send_part.at[step], recv_sem=recv_part.at[step],
            device_id=(target, imp), device_id_type=pl.DeviceIdType.MESH,
        )

    def lse_copy(step, k, target):
        return pltpu.make_async_remote_copy(
            src_ref=lses.at[step, k], dst_ref=lses.at[step, k],
            send_sem=send_lse.at[step], recv_sem=recv_lse.at[step, k // batch],
            device_id=(target, imp), device_id_type=pl.DeviceIdType.MESH,
        )

    def spend_copy(step, source, target):
        return pltpu.make_async_remote_copy(
            src_ref=spends.at[step, source], dst_ref=spends.at[step, source],
            send_sem=send_spend.at[step, target], recv_sem=recv_spend.at[step, source],
            device_id=(adv, target), device_id_type=pl.DeviceIdType.MESH,
        )

    is_owner = base * stride == adv

    def bit_steps(own, size):
        return [(1 - 2 * lax.rem(lax.div(own, 1 << i), 2)) << i for i in range(size.bit_length() - 1)]

    def partner(own, steps, c, size):
        if size & (size - 1):
            return lax.rem(own + c, size)
        if isinstance(c, int):
            return own + sum((step for i, step in enumerate(steps) if c >> i & 1), 0)
        return own + sum((step * lax.rem(lax.div(c, 1 << i), 2) for i, step in enumerate(steps)), 0)

    groups = owners // batch
    home, seat = lax.div(base, batch), lax.rem(base, batch)
    home_steps, seat_steps = bit_steps(home, groups), bit_steps(seat, batch)
    adv_steps = bit_steps(adv, n)

    def members(b):
        first = partner(home, home_steps, groups - 1 - b, groups) * batch
        return [first + partner(seat, seat_steps, batch - 1 - g, batch) for g in range(batch)]

    def drain(ref, sem, most):
        def wait(count):
            blocks = ref.at[pl.ds(0, count)]
            pltpu.make_async_copy(blocks, blocks, sem).wait()

        if stride == 1:
            wait(most - 1)
        else:
            pl.when(is_owner)(lambda: wait(most - 1))
            pl.when(jnp.logical_not(is_owner))(lambda: wait(most))

    def if_owner(run):
        if stride == 1:
            run()
        else:
            pl.when(is_owner)(run)

    small = [
        pltpu.make_async_copy(source, target, small_sem.at[at])
        for at, (source, target) in enumerate(((start, pace_row), (limits, limit_row), (reserve, floors)))
    ]
    small[0].start()

    for k in members(0):
        load(k).start()

    barrier = pltpu.get_barrier_semaphore()

    @pl.loop(1, n, unroll=True)
    def _(t):
        pl.semaphore_signal(
            barrier, inc=1, device_id=(lax.rem(adv + t, n), imp), device_id_type=pl.DeviceIdType.MESH
        )

    @pl.loop(1, m, unroll=True)
    def _(t):
        pl.semaphore_signal(
            barrier, inc=1, device_id=(adv, lax.rem(imp + t, m)), device_id_type=pl.DeviceIdType.MESH
        )

    @pl.loop(1, groups)
    def _(b):
        for k in members(b):
            load(k).start()

    small[1].start()
    small[2].start()

    def set_column():
        for h in range(halves):
            spread = jnp.broadcast_to(pace_row[h : h + 1, :], (LANES, LANES)).T * SCALE
            column[h * LANES : (h + 1) * LANES, :] = spread
            column16[h * LANES : (h + 1) * LANES, :] = spread.astype(jnp.bfloat16)

    small[0].wait()
    set_column()

    price_copy = pltpu.make_async_copy(price_row, price_out, out_sem.at[0])

    tall = math.gcd(rows, TALL)
    blocks = [slice(at, at + tall) for at in range(0, rows, tall)]

    def segment(step, k):
        for r in range(wide):
            lanes = slice(r * LANES, (r + 1) * LANES)
            rough = held[k, blocks[0], lanes] * column16[blocks[0], :]
            for block in blocks[1:]:
                rough = jnp.maximum(rough, held[k, block, lanes] * column16[block, :])
            top = jnp.max(rough.astype(jnp.float32), axis=0, keepdims=True)
            tally = jnp.zeros((8, LANES), jnp.float32)
            for block in blocks:
                value = held[k, block, lanes].astype(jnp.float32)
                scaled = jnp.exp2(value * column[block, :] - top)
                weighted[k, block, lanes] = scaled * value
                tally = tally + jnp.sum(scaled.reshape(-1, 8, LANES), axis=0)
            tops[k, r : r + 1, :] = top
            mine[step, k, r : r + 1, :] = (
                top + jnp.log(jnp.sum(tally, axis=0, keepdims=True)) * LOG2E
            )

    @pl.loop(0, ROUNDS)
    def _(step):
        @pl.loop(0, groups)
        def _(b):
            ks = members(b)

            @pl.when(step == 0)
            def _():
                for k in ks:
                    load(k).wait()

            for k in ks:
                segment(step, k)

            @pl.when(jnp.logical_and(step == 0, b == 0))
            def _():
                pl.semaphore_wait(barrier, n - 1 + m - 1)

            for k in ks[:-1]:
                part_copy(step, k, adv, k * stride).start()
            pl.when(ks[-1] * stride != adv)(part_copy(step, ks[-1], adv, ks[-1] * stride).start)

        @pl.when(step == 0)
        def _():
            small[1].wait()
            small[2].wait()

        def own():
            parts[step, adv] = mine[step, base]
            blocks = parts.at[step, pl.ds(0, n - 1)]
            pltpu.make_async_copy(blocks, blocks, recv_part.at[step]).wait()
            every = parts[step]
            floor = floors[base] * SCALE
            upper = jnp.maximum(jnp.max(every, axis=0), floor)
            whole = jnp.sum(jnp.exp2(every - upper[None]), axis=0) + jnp.exp2(floor - upper)
            lses[step, base] = upper + jnp.log(whole) * LOG2E

            for c in range(n - 1, 0, -1):
                lse_copy(step, base, partner(adv, adv_steps, c, n)).start()

        if_owner(own)
        drain(mine.at[step], send_part.at[step], owners)
        def gather(c, total):
            group = partner(home, home_steps, c, groups)
            first = group * batch

            @pl.when(c == 0)
            def _():
                drain(lses.at[step], recv_lse.at[step, group], batch)

            @pl.when(c > 0)
            def _():
                every = lses.at[step, pl.ds(0, batch)]
                pltpu.make_async_copy(every, every, recv_lse.at[step, group]).wait()

            here = pl.ds(first, batch)
            shares[...] = jnp.exp2(tops[here] - lses[step, here])
            sums = []
            for block, part in zip(blocks, total):
                for g in range(batch):
                    for r in range(wide):
                        lanes = slice(r * LANES, (r + 1) * LANES)
                        part = part + weighted[first + g, block, lanes] * shares[g, r : r + 1, :]
                sums.append(part)
            return tuple(sums)

        nothing = jnp.zeros((tall, LANES), jnp.float32)
        total = lax.fori_loop(0, groups, gather, (nothing,) * len(blocks))
        total = jnp.concatenate(total, axis=0)
        for h in range(halves):
            spends[step, imp, h : h + 1, :] = jnp.sum(
                total[h * LANES : (h + 1) * LANES, :].T, axis=0, keepdims=True
            )

        @pl.loop(1, m)
        def _(t):
            spend_copy(step, imp, lax.rem(imp + t, m)).start()

        @pl.when(step == ROUNDS - 1)
        def _():
            price_row[...] = lses[step] * (EPS * LN2)
            price_copy.start()

        def sent():
            blocks = parts.at[step, pl.ds(0, n - 1)]
            pltpu.make_async_copy(blocks, blocks, send_lse.at[step]).wait()

        if_owner(sent)

        @pl.loop(1, m)
        def _(t):
            spend_copy(step, lax.rem(imp + t, m), imp).wait_recv()

        spend = pace_row[...] * jnp.sum(spends[step], axis=0)
        pace_row[...] = jnp.minimum(1.0, pace_row[...] * jnp.sqrt(limit_row[...] / spend))
        pl.when(step < ROUNDS - 1)(set_column)

    pace_copy = pltpu.make_async_copy(pace_row, pace_out, out_sem.at[1])
    pace_copy.start()
    for step in range(ROUNDS):

        @pl.loop(1, m)
        def _(t):
            spend_copy(step, imp, lax.rem(imp + t, m)).wait_send()

    price_copy.wait()
    pace_copy.wait()


def hand_over(pace, prices, pace_out, price_out):
    pace_out[...] = pace[...]
    price_out[...] = prices[...]


def on_device(n, m, values, limits, start_pace, reserve):
    rows, columns = values.shape
    tiles = columns // LANES
    owners = math.gcd(n, tiles)
    wide = tiles // owners
    halves = rows // LANES
    batch = math.gcd(owners, BATCH)
    vmem = pl.BlockSpec(memory_space=pltpu.VMEM)
    away = pl.BlockSpec(memory_space=pltpu.HBM)
    f32 = jnp.float32
    pace, prices = pl.pallas_call(
        functools.partial(kernel, n, m, owners),
        out_shape=(
            jax.ShapeDtypeStruct((halves, LANES), f32),
            jax.ShapeDtypeStruct((owners, wide, LANES), f32),
        ),
        in_specs=[away] * 4,
        out_specs=(away, away),
        scratch_shapes=[
            pltpu.VMEM((owners, rows, wide * LANES), jnp.bfloat16),
            pltpu.VMEM((owners, rows, wide * LANES), f32),
            pltpu.VMEM((rows, LANES), f32),
            pltpu.VMEM((rows, LANES), jnp.bfloat16),
            pltpu.VMEM((halves, LANES), f32),
            pltpu.VMEM((halves, LANES), f32),
            pltpu.VMEM((owners, wide, LANES), f32),
            pltpu.VMEM((owners, wide, LANES), f32),
            pltpu.VMEM((owners, wide, LANES), f32),
            pltpu.VMEM((batch, wide, LANES), f32),
            pltpu.VMEM((ROUNDS, owners, wide, LANES), f32),
            pltpu.VMEM((ROUNDS, n, wide, LANES), f32),
            pltpu.VMEM((ROUNDS, owners, wide, LANES), f32),
            pltpu.VMEM((ROUNDS, m, halves, LANES), f32),
            pltpu.SemaphoreType.DMA((3,)),
            pltpu.SemaphoreType.DMA((2,)),
            pltpu.SemaphoreType.DMA((owners,)),
            pltpu.SemaphoreType.DMA((ROUNDS,)),
            pltpu.SemaphoreType.DMA((ROUNDS,)),
            pltpu.SemaphoreType.DMA((ROUNDS,)),
            pltpu.SemaphoreType.DMA((ROUNDS, owners // batch)),
            pltpu.SemaphoreType.DMA((ROUNDS, m)),
            pltpu.SemaphoreType.DMA((ROUNDS, m)),
        ],
        compiler_params=pltpu.CompilerParams(
            collective_id=0, has_side_effects=True, vmem_limit_bytes=62 * 2**20
        ),
        name="pacing",
    )(
        values,
        limits.reshape(halves, LANES),
        start_pace.reshape(halves, LANES),
        reserve.reshape(owners, wide, LANES),
    )
    pace, prices = pl.pallas_call(
        hand_over,
        out_shape=(
            jax.ShapeDtypeStruct(pace.shape, f32),
            jax.ShapeDtypeStruct(prices.shape, f32),
        ),
        in_specs=[vmem, vmem],
        out_specs=(vmem, vmem),
        compiler_params=pltpu.CompilerParams(vmem_limit_bytes=62 * 2**20),
        name="hand_over",
    )(pace, prices)
    return pace.reshape(rows), prices.reshape(columns)


def solution(mesh):
    placed = (P("adv", "imp"), P("adv"), P("adv"), P("imp"))
    body = functools.partial(on_device, mesh.shape["adv"], mesh.shape["imp"])
    return jax.shard_map(
        body, mesh=mesh, in_specs=placed, out_specs=(P("adv"), P("imp")), check_vma=False
    )
```

```python
import functools
import math

import jax
import jax.numpy as jnp
from jax import lax
from jax.experimental import pallas as pl
from jax.experimental.pallas import tpu as pltpu
from jax.sharding import PartitionSpec as P

ROUNDS = 2
EPS = 0.015
LANES = 128
BATCH = 2
TALL = 64
LOG2E = math.log2(math.e)
LN2 = math.log(2.0)
SCALE = LOG2E / EPS


def kernel(
    n, m, owners,
    values, limits, start, reserve,
    pace_out, price_out,
    held, weighted, column, column16, pace_row, limit_row, floors, price_row, tops, shares, mine, parts, lses, spends,
    small_sem, out_sem, load_sem, send_part, recv_part, send_lse, recv_lse, send_spend, recv_spend,
):
    adv, imp = lax.axis_index("adv"), lax.axis_index("imp")
    stride = n // owners
    base = adv // stride
    segs, rows, width = held.shape
    wide = width // LANES
    halves = rows // LANES
    batch = math.gcd(owners, BATCH)

    def load(k):
        return pltpu.make_async_copy(
            values.at[:, pl.ds(pl.multiple_of(k * width, width), width)], held.at[k], load_sem.at[k]
        )

    def part_copy(step, k, source, target):
        return pltpu.make_async_remote_copy(
            src_ref=mine.at[step, k], dst_ref=parts.at[step, source],
            send_sem=send_part.at[step], recv_sem=recv_part.at[step],
            device_id=(target, imp), device_id_type=pl.DeviceIdType.MESH,
        )

    def lse_copy(step, k, target):
        return pltpu.make_async_remote_copy(
            src_ref=lses.at[step, k], dst_ref=lses.at[step, k],
            send_sem=send_lse.at[step], recv_sem=recv_lse.at[step, k // batch],
            device_id=(target, imp), device_id_type=pl.DeviceIdType.MESH,
        )

    def spend_copy(step, source, target):
        return pltpu.make_async_remote_copy(
            src_ref=spends.at[step, source], dst_ref=spends.at[step, source],
            send_sem=send_spend.at[step, target], recv_sem=recv_spend.at[step, source],
            device_id=(adv, target), device_id_type=pl.DeviceIdType.MESH,
        )

    is_owner = base * stride == adv

    def bit_steps(own, size):
        return [(1 - 2 * lax.rem(lax.div(own, 1 << i), 2)) << i for i in range(size.bit_length() - 1)]

    def partner(own, steps, c, size):
        if size & (size - 1):
            return lax.rem(own + c, size)
        if isinstance(c, int):
            return own + sum((step for i, step in enumerate(steps) if c >> i & 1), 0)
        return own + sum((step * lax.rem(lax.div(c, 1 << i), 2) for i, step in enumerate(steps)), 0)

    groups = owners // batch
    late = max(groups // 2 - 1, 0)
    home, seat = lax.div(base, batch), lax.rem(base, batch)
    home_steps, seat_steps = bit_steps(home, groups), bit_steps(seat, batch)
    adv_steps = bit_steps(adv, n)

    def members(b):
        first = partner(home, home_steps, groups - 1 - b, groups) * batch
        return [first + partner(seat, seat_steps, batch - 1 - g, batch) for g in range(batch)]

    def drain(ref, sem, most):
        def wait(count):
            blocks = ref.at[pl.ds(0, count)]
            pltpu.make_async_copy(blocks, blocks, sem).wait()

        if stride == 1:
            wait(most - 1)
        else:
            pl.when(is_owner)(lambda: wait(most - 1))
            pl.when(jnp.logical_not(is_owner))(lambda: wait(most))

    def if_owner(run):
        if stride == 1:
            run()
        else:
            pl.when(is_owner)(run)

    small = [
        pltpu.make_async_copy(source, target, small_sem.at[at])
        for at, (source, target) in enumerate(((start, pace_row), (limits, limit_row), (reserve, floors)))
    ]
    small[0].start()

    for k in members(0):
        load(k).start()

    barrier = pltpu.get_barrier_semaphore()

    @pl.loop(1, n, unroll=True)
    def _(t):
        pl.semaphore_signal(
            barrier, inc=1, device_id=(lax.rem(adv + t, n), imp), device_id_type=pl.DeviceIdType.MESH
        )

    @pl.loop(1, m, unroll=True)
    def _(t):
        pl.semaphore_signal(
            barrier, inc=1, device_id=(adv, lax.rem(imp + t, m)), device_id_type=pl.DeviceIdType.MESH
        )

    @pl.loop(1, groups)
    def _(b):
        for k in members(b):
            load(k).start()

    small[1].start()
    small[2].start()

    def set_column():
        for h in range(halves):
            spread = jnp.broadcast_to(pace_row[h : h + 1, :], (LANES, LANES)).T * SCALE
            column[h * LANES : (h + 1) * LANES, :] = spread
            column16[h * LANES : (h + 1) * LANES, :] = spread.astype(jnp.bfloat16)

    small[0].wait()
    set_column()

    price_copy = pltpu.make_async_copy(price_row, price_out, out_sem.at[0])

    tall = math.gcd(rows, TALL)
    blocks = [slice(at, at + tall) for at in range(0, rows, tall)]

    def segment(step, k):
        for r in range(wide):
            lanes = slice(r * LANES, (r + 1) * LANES)
            rough = held[k, blocks[0], lanes] * column16[blocks[0], :]
            for block in blocks[1:]:
                rough = jnp.maximum(rough, held[k, block, lanes] * column16[block, :])
            top = jnp.max(rough.astype(jnp.float32), axis=0, keepdims=True)
            tally = jnp.zeros((8, LANES), jnp.float32)
            for block in blocks:
                value = held[k, block, lanes].astype(jnp.float32)
                scaled = jnp.exp2(value * column[block, :] - top)
                weighted[k, block, lanes] = scaled * value
                tally = tally + jnp.sum(scaled.reshape(-1, 8, LANES), axis=0)
            tops[k, r : r + 1, :] = top
            mine[step, k, r : r + 1, :] = (
                top + jnp.log(jnp.sum(tally, axis=0, keepdims=True)) * LOG2E
            )

    @pl.loop(0, ROUNDS)
    def _(step):
        @pl.loop(0, groups)
        def _(b):
            ks = members(b)

            @pl.when(step == 0)
            def _():
                for k in ks:
                    load(k).wait()

            for k in ks:
                segment(step, k)

            @pl.when(jnp.logical_and(step == 0, b == late))
            def _():
                pl.semaphore_wait(barrier, n - 1 + m - 1)

                @pl.loop(0, late)
                def _(e):
                    for k in members(e):
                        part_copy(step, k, adv, k * stride).start()

            @pl.when(jnp.logical_or(step > 0, b >= late))
            def _():
                for k in ks[:-1]:
                    part_copy(step, k, adv, k * stride).start()
                pl.when(ks[-1] * stride != adv)(part_copy(step, ks[-1], adv, ks[-1] * stride).start)

        @pl.when(step == 0)
        def _():
            small[1].wait()
            small[2].wait()

        def own():
            parts[step, adv] = mine[step, base]
            blocks = parts.at[step, pl.ds(0, n - 1)]
            pltpu.make_async_copy(blocks, blocks, recv_part.at[step]).wait()
            every = parts[step]
            floor = floors[base] * SCALE
            upper = jnp.maximum(jnp.max(every, axis=0), floor)
            whole = jnp.sum(jnp.exp2(every - upper[None]), axis=0) + jnp.exp2(floor - upper)
            lses[step, base] = upper + jnp.log(whole) * LOG2E

            for c in range(n - 1, 0, -1):
                lse_copy(step, base, partner(adv, adv_steps, c, n)).start()

        if_owner(own)
        drain(mine.at[step], send_part.at[step], owners)
        def gather(c, total):
            group = partner(home, home_steps, c, groups)
            first = group * batch

            @pl.when(c == 0)
            def _():
                drain(lses.at[step], recv_lse.at[step, group], batch)

            @pl.when(c > 0)
            def _():
                every = lses.at[step, pl.ds(0, batch)]
                pltpu.make_async_copy(every, every, recv_lse.at[step, group]).wait()

            here = pl.ds(first, batch)
            shares[...] = jnp.exp2(tops[here] - lses[step, here])
            sums = []
            for block, part in zip(blocks, total):
                for g in range(batch):
                    for r in range(wide):
                        lanes = slice(r * LANES, (r + 1) * LANES)
                        part = part + weighted[first + g, block, lanes] * shares[g, r : r + 1, :]
                sums.append(part)
            return tuple(sums)

        nothing = jnp.zeros((tall, LANES), jnp.float32)
        total = lax.fori_loop(0, groups, gather, (nothing,) * len(blocks))
        total = jnp.concatenate(total, axis=0)
        for h in range(halves):
            spends[step, imp, h : h + 1, :] = jnp.sum(
                total[h * LANES : (h + 1) * LANES, :].T, axis=0, keepdims=True
            )

        @pl.loop(1, m)
        def _(t):
            spend_copy(step, imp, lax.rem(imp + t, m)).start()

        @pl.when(step == ROUNDS - 1)
        def _():
            price_row[...] = lses[step] * (EPS * LN2)
            price_copy.start()

        def sent():
            blocks = parts.at[step, pl.ds(0, n - 1)]
            pltpu.make_async_copy(blocks, blocks, send_lse.at[step]).wait()

        if_owner(sent)

        @pl.loop(1, m)
        def _(t):
            spend_copy(step, lax.rem(imp + t, m), imp).wait_recv()

        spend = pace_row[...] * jnp.sum(spends[step], axis=0)
        pace_row[...] = jnp.minimum(1.0, pace_row[...] * jnp.sqrt(limit_row[...] / spend))
        pl.when(step < ROUNDS - 1)(set_column)

    pace_copy = pltpu.make_async_copy(pace_row, pace_out, out_sem.at[1])
    pace_copy.start()
    for step in range(ROUNDS):

        @pl.loop(1, m)
        def _(t):
            spend_copy(step, imp, lax.rem(imp + t, m)).wait_send()

    price_copy.wait()
    pace_copy.wait()


def hand_over(pace, prices, pace_out, price_out):
    pace_out[...] = pace[...]
    price_out[...] = prices[...]


def on_device(n, m, values, limits, start_pace, reserve):
    rows, columns = values.shape
    tiles = columns // LANES
    owners = math.gcd(n, tiles)
    wide = tiles // owners
    halves = rows // LANES
    batch = math.gcd(owners, BATCH)
    vmem = pl.BlockSpec(memory_space=pltpu.VMEM)
    away = pl.BlockSpec(memory_space=pltpu.HBM)
    f32 = jnp.float32
    pace, prices = pl.pallas_call(
        functools.partial(kernel, n, m, owners),
        out_shape=(
            jax.ShapeDtypeStruct((halves, LANES), f32),
            jax.ShapeDtypeStruct((owners, wide, LANES), f32),
        ),
        in_specs=[away] * 4,
        out_specs=(away, away),
        scratch_shapes=[
            pltpu.VMEM((owners, rows, wide * LANES), jnp.bfloat16),
            pltpu.VMEM((owners, rows, wide * LANES), f32),
            pltpu.VMEM((rows, LANES), f32),
            pltpu.VMEM((rows, LANES), jnp.bfloat16),
            pltpu.VMEM((halves, LANES), f32),
            pltpu.VMEM((halves, LANES), f32),
            pltpu.VMEM((owners, wide, LANES), f32),
            pltpu.VMEM((owners, wide, LANES), f32),
            pltpu.VMEM((owners, wide, LANES), f32),
            pltpu.VMEM((batch, wide, LANES), f32),
            pltpu.VMEM((ROUNDS, owners, wide, LANES), f32),
            pltpu.VMEM((ROUNDS, n, wide, LANES), f32),
            pltpu.VMEM((ROUNDS, owners, wide, LANES), f32),
            pltpu.VMEM((ROUNDS, m, halves, LANES), f32),
            pltpu.SemaphoreType.DMA((3,)),
            pltpu.SemaphoreType.DMA((2,)),
            pltpu.SemaphoreType.DMA((owners,)),
            pltpu.SemaphoreType.DMA((ROUNDS,)),
            pltpu.SemaphoreType.DMA((ROUNDS,)),
            pltpu.SemaphoreType.DMA((ROUNDS,)),
            pltpu.SemaphoreType.DMA((ROUNDS, owners // batch)),
            pltpu.SemaphoreType.DMA((ROUNDS, m)),
            pltpu.SemaphoreType.DMA((ROUNDS, m)),
        ],
        compiler_params=pltpu.CompilerParams(
            collective_id=0, has_side_effects=True, vmem_limit_bytes=62 * 2**20
        ),
        name="pacing",
    )(
        values,
        limits.reshape(halves, LANES),
        start_pace.reshape(halves, LANES),
        reserve.reshape(owners, wide, LANES),
    )
    pace, prices = pl.pallas_call(
        hand_over,
        out_shape=(
            jax.ShapeDtypeStruct(pace.shape, f32),
            jax.ShapeDtypeStruct(prices.shape, f32),
        ),
        in_specs=[vmem, vmem],
        out_specs=(vmem, vmem),
        compiler_params=pltpu.CompilerParams(vmem_limit_bytes=62 * 2**20),
        name="hand_over",
    )(pace, prices)
    return pace.reshape(rows), prices.reshape(columns)


def solution(mesh):
    placed = (P("adv", "imp"), P("adv"), P("adv"), P("imp"))
    body = functools.partial(on_device, mesh.shape["adv"], mesh.shape["imp"])
    return jax.shard_map(
        body, mesh=mesh, in_specs=placed, out_specs=(P("adv"), P("imp")), check_vma=False
    )
```
